128 devices in a mesh: req: 32 (over z, y, core), head: 4 (over x).
Axes of the slice: x: 4, y: 4, z: 4, core: 2. Of those that a mesh axis runs over, the one named last changes fastest.
Arguments:
- queries: bfloat16 [98304, 8, 128], P('req', 'head'), may hold values from -6 to 6
- key_rows: bfloat16 [98304, 8, 128], P('req', 'head'), may hold values from -6 to 6
- values: bfloat16 [98304, 16, 128], P('req', 'head'), may hold values from -6 to 6
- gate_input: bfloat16 [98304, 16, 128], P('req', 'head'), may hold values from -6 to 6
- write_rate: float32 [98304, 16], P('req', 'head'), may hold values from 0.1 to 0.9
- log_decay: float32 [98304, 16], P('req', 'head'), may hold values from -1 to 0
- norm_gain: float32 [128], replicated, may hold values from 0.1 to 1.9
- out_weight: bfloat16 [2048, 2048], P('head'), may hold values from -0.125 to 0.125
- cache_states: float32 [256, 16, 128, 128], P('req', 'head'), may hold values from -6 to 6
- cache_owner: int32 [768], replicated, may hold values from 0 to 31, as said below
- cache_slot: int32 [768], replicated, may hold values from 0 to 7
- suffix_blocks: int32 [768], replicated, may hold values from 1 to 2, as said below
- new_slot: int32 [768], replicated, may hold values from 0 to 23, as said below
Outputs:
- layer_out: bfloat16 [98304, 2048], P(('req', 'head'))
- new_cache: float32 [768, 16, 128, 128], P('req', 'head')
The draws below stay inside these ranges and needn't reach their ends.
Inputs may be any that keep to these rules, and one draw needn't show every extreme that they name: `cache_owner`: the 24 requests of one device name one owner at most 1 times, and some owner that many times; for every position within a device's requests, each owner is named by exactly one device, so each owner is named by exactly 24 requests. `suffix_blocks`: the largest, 2, is reached. `new_slot`: the 24 requests that name one owner take its 24 new slots one each.
All inputs are finite; a program needn't handle non-finite values.
Results may differ from the reference program's by a relative error of at most 0.019.
Values may be sent and summed in bfloat16 or wider, within the bound.
No kernel may reach another device: no remote copies, remote signals or barrier semaphores. Data moves between devices by JAX's collectives and lax.ppermute only.
A program may use at most 256 MiB of HBM per device.

```python
import math
import jax
import jax.numpy as jnp
from jax import lax

D = 2048
OUTPUT_CHANNELS = 16
HK = 8
DK = 128
DV = 128
BLOCK = 64
TAIL_POSITIONS = 128
REQ_DEV = 24
SLOTS_DEV = 8
NBLK = 2
REQS = 768
TOKENS = 98304
HV_DEV = 4
CACHE_SLOTS = 256
NEW_SLOTS = 768
N_REQ = 32
N_HEAD = 4


def owner_table(key):
    labels = jax.random.permutation(jax.random.fold_in(key, 11), N_REQ)
    placed = jax.random.permutation(jax.random.fold_in(key, 12), N_REQ)
    shifts = jax.random.permutation(jax.random.fold_in(key, 13), N_REQ)
    device_ids = jnp.arange(N_REQ, dtype=jnp.int32)[:, None]
    positions = jnp.arange(REQ_DEV, dtype=jnp.int32)[None, :]
    mixed_ids = (placed[device_ids] + shifts[positions % N_REQ]) % N_REQ
    return labels[mixed_ids].reshape(-1).astype(jnp.int32)


def draw_cache_owner(key, part):
    return owner_table(key)


def draw_new_slot(key, part):
    owners = owner_table(key)
    key = jax.random.fold_in(key, 5)
    subkeys = jax.random.split(key, N_REQ)
    orders = jax.vmap(lambda subkey: jax.random.permutation(subkey, REQ_DEV))(subkeys)
    positions = jnp.arange(REQ_DEV * N_REQ, dtype=jnp.int32) % REQ_DEV
    return orders[owners, positions].astype(jnp.int32)


def draw_suffix_blocks(key, part):
    key = jax.random.fold_in(key, 7)
    heavy = jax.random.randint(jax.random.fold_in(key, 1), (N_REQ, 1), 0, 4) == 0
    light_cap = jax.random.randint(jax.random.fold_in(key, 2), (N_REQ, 1), 1, 3)
    light = jax.random.randint(jax.random.fold_in(key, 3), (N_REQ, REQ_DEV), 0, 1000) % light_cap + 1
    longer = jax.random.randint(jax.random.fold_in(key, 4), (N_REQ, REQ_DEV), 1, NBLK + 1)
    blocks = jnp.where(heavy, longer, jnp.minimum(light, NBLK)).reshape(-1)
    chosen = jax.random.randint(jax.random.fold_in(key, 6), (), 0, N_REQ * REQ_DEV)
    return blocks.at[chosen].set(NBLK).astype(jnp.int32)


def draw_log_decay(key, part):
    key = jax.random.fold_in(key, 9)
    overall_aggregate = REQ_DEV * N_REQ
    upper = 1.0 / 25.0
    lower = 0.2 / TAIL_POSITIONS
    channelwise_speed = jnp.exp(jax.random.uniform(jax.random.fold_in(key, 1), (1, 1, OUTPUT_CHANNELS), jnp.float32, math.log(lower), math.log(upper)))
    query_batch_factor = jnp.exp(jax.random.uniform(jax.random.fold_in(key, 2), (overall_aggregate, 1, 1), jnp.float32, math.log(0.5), math.log(2.0)))
    position_scaling_factor = jnp.exp(jax.random.uniform(jax.random.fold_in(key, 3), (overall_aggregate, TAIL_POSITIONS, OUTPUT_CHANNELS), jnp.float32, math.log(0.5), math.log(2.0)))
    spike_sequence = jax.random.uniform(jax.random.fold_in(key, 4), (overall_aggregate, TAIL_POSITIONS, OUTPUT_CHANNELS), jnp.float32) < 3.0 / TAIL_POSITIONS
    penalty_entries = jnp.log(jax.random.uniform(jax.random.fold_in(key, 5), (overall_aggregate, TAIL_POSITIONS, OUTPUT_CHANNELS), jnp.float32, 0.5, 0.8))
    speed_entries = -channelwise_speed * query_batch_factor * position_scaling_factor + jnp.where(spike_sequence, penalty_entries, 0.0)
    return speed_entries.reshape(overall_aggregate * TAIL_POSITIONS, OUTPUT_CHANNELS).astype(jnp.float32)


def set_ends(array, rng, low, top_value):
    longest = array.shape.index(max(array.shape))
    spots = []
    for shift in (0, 1):
        where = [jax.random.randint(jax.random.fold_in(rng, axis), (), 0, length) for axis, length in enumerate(array.shape)]
        where[longest] = (where[longest] + shift) % array.shape[longest]
        spots.append(tuple(where))
    return array.at[spots[0]].set(low).at[spots[1]].set(top_value)


def levels(rng, extent, cuts, low, top_value):
    factor_of = 1.0
    for dim, shards_of in cuts:
        heights = jax.random.uniform(jax.random.fold_in(jax.random.fold_in(rng, 6), dim), (shards_of,), jnp.float32, low / len(cuts), top_value / len(cuts))
        factor_of = factor_of * jnp.repeat(jnp.exp(heights), extent[dim] // shards_of).reshape((-1,) + (1,) * (len(extent) - 1 - dim))
    return factor_of


def scatter_about(key, dims, width, bound, cuts=(), kind=jnp.bfloat16):
    entries = width * jax.random.normal(key, dims, jnp.float32)
    if cuts:
        entries = entries * levels(key, dims, cuts, -0.22, 0.18)
    return jnp.clip(entries, -bound, bound).astype(kind)


def setup_inputs(seed: int = 0) -> dict:
    keys = jax.random.split(jax.random.key(seed), 14)
    queries = scatter_about(keys[0], (TOKENS, HK, DK), 1.0, 6.0, ((0, 32), (1, 4)))
    key_rows = scatter_about(keys[1], (TOKENS, HK, DK), 1.0, 6.0, ((0, 32), (1, 4)))
    values = scatter_about(keys[2], (TOKENS, OUTPUT_CHANNELS, DV), 1.0, 6.0, ((0, 32), (1, 4)))
    gate_input = scatter_about(keys[3], (TOKENS, OUTPUT_CHANNELS, DV), 1.0, 6.0, ((0, 32), (1, 4)))
    write_rate = jnp.clip(0.1 + 0.79999997 * jax.random.uniform(keys[4], (TOKENS, OUTPUT_CHANNELS), jnp.float32) ** levels(keys[4], (TOKENS, OUTPUT_CHANNELS), ((0, 32), (1, 4)), -0.2, 0.2), 0.1, 0.9)
    log_decay = draw_log_decay(jax.random.fold_in(keys[13], 71), 0)
    norm_gain = jnp.clip(1.0 + 0.18 * jax.random.normal(keys[6], (DV,), jnp.float32), 0.1, 1.9)
    out_weight = scatter_about(keys[7], (OUTPUT_CHANNELS * DV, D), (OUTPUT_CHANNELS * DV) ** -0.5, 0.125, ((0, 4),))
    cache_states = scatter_about(keys[8], (CACHE_SLOTS, OUTPUT_CHANNELS, DK, DV), 1.0, 6.0, ((0, 32), (1, 4)), jnp.float32)
    cache_owner = draw_cache_owner(jax.random.fold_in(keys[13], 71), 0)
    cache_slot = set_ends(jax.random.randint(keys[10], (REQS,), 0, SLOTS_DEV), jax.random.fold_in(keys[10], 1), 0, SLOTS_DEV - 1).astype(jnp.int32)
    suffix_blocks = draw_suffix_blocks(jax.random.fold_in(keys[13], 71), 0)
    new_slot = draw_new_slot(jax.random.fold_in(keys[13], 71), 0)
    return dict(queries=queries, key_rows=key_rows, values=values, gate_input=gate_input, write_rate=write_rate, log_decay=log_decay, norm_gain=norm_gain, out_weight=out_weight, cache_states=cache_states, cache_owner=cache_owner, cache_slot=cache_slot, suffix_blocks=suffix_blocks, new_slot=new_slot)


HIGHEST = lax.Precision.HIGHEST
EPSILON = 1e-06

def unit_rows(vectors):
    vectors = vectors.astype(jnp.float32)
    return vectors * lax.rsqrt(lax.optimization_barrier(jnp.sum(vectors * vectors, axis=-1, keepdims=True)) + EPSILON)

def prepare(queries, key_rows, values, write_rate, log_decay):
    steps_in = log_decay.shape[-1]
    query_wide = queries.astype(jnp.float32)
    key_wide = key_rows.astype(jnp.float32)
    running = jnp.cumsum(log_decay, axis=-1)
    row_ids = lax.broadcasted_iota(jnp.int32, (steps_in, steps_in), 0)
    col_ids = lax.broadcasted_iota(jnp.int32, (steps_in, steps_in), 1)
    spacing = running[..., :, None] - running[..., None, :]
    strict = row_ids > col_ids
    within = row_ids >= col_ids
    fade_strict = jnp.where(strict, jnp.exp(jnp.where(strict, spacing, 0.0)), 0.0)
    fade_within = jnp.where(within, jnp.exp(jnp.where(within, spacing, 0.0)), 0.0)
    affinity = jnp.einsum('...td,...sd->...ts', key_rows.astype(jnp.float32), key_rows.astype(jnp.float32), preferred_element_type=jnp.float32)
    system = write_rate[..., :, None] * affinity * fade_strict + jnp.eye(steps_in, dtype=jnp.float32)
    growth = jnp.exp(running)
    targets = jnp.concatenate([write_rate[..., None] * values, (write_rate * growth)[..., None] * key_wide], axis=-1)
    solved = lax.linalg.triangular_solve(system, targets, left_side=True, lower=True, unit_diagonal=True)
    value_width = values.shape[-1]
    corrected = solved[..., :value_width]
    projector = solved[..., value_width:]
    scores = jnp.einsum('...td,...sd->...ts', queries.astype(jnp.float32), key_rows.astype(jnp.float32), preferred_element_type=jnp.float32) * fade_within
    query_fade = query_wide * growth[..., None]
    ending = running[..., -1:]
    key_fade = key_wide * jnp.exp(ending - running)[..., None]
    return (query_fade, key_fade, corrected, projector, scores, jnp.exp(ending[..., 0]))

def advance(carried, query_fade, key_fade, corrected, projector, scores, retained):
    fresh_values = corrected - jnp.einsum('...tk,...kv->...tv', projector, carried, precision=HIGHEST)
    block_out = jnp.einsum('...tk,...kv->...tv', query_fade, carried, precision=HIGHEST)
    block_out = block_out + jnp.einsum('...ts,...sv->...tv', scores, fresh_values, precision=HIGHEST)
    updated = retained[..., None, None] * carried + jnp.einsum('...tk,...tv->...kv', key_fade, fresh_values, precision=HIGHEST)
    return (block_out, updated)

def reference(queries, key_rows, values, gate_input, write_rate, log_decay, norm_gain, out_weight, cache_states, cache_owner, cache_slot, suffix_blocks, new_slot):
    repeats = OUTPUT_CHANNELS // HK
    blocks_per = TAIL_POSITIONS // BLOCK
    group_width = HV_DEV * DV
    weight_groups = out_weight.reshape(N_HEAD, group_width, D).astype(jnp.float32)
    slot_index = (cache_owner * SLOTS_DEV + cache_slot).astype(jnp.int32)

    def arrange(source):
        shaped = source.reshape((blocks_per, BLOCK) + source.shape[1:])
        if shaped.ndim == 4:
            return jnp.transpose(shaped, (2, 0, 1, 3))
        return jnp.transpose(shaped, (2, 0, 1))

    def serve(packed):
        query_part, key_part, value_part, gate_part, rate_part, decay_part, slot_pick, block_total = packed
        query_short = (jnp.repeat(unit_rows(query_part), repeats, axis=1) * DK ** (-0.5)).astype(jnp.bfloat16)
        key_short = jnp.repeat(unit_rows(key_part), repeats, axis=1).astype(jnp.bfloat16)
        ready = prepare(arrange(query_short), arrange(key_short), arrange(value_part.astype(jnp.float32)), arrange(rate_part), arrange(decay_part))
        initial = lax.dynamic_index_in_dim(cache_states, slot_pick, 0, keepdims=False)

        def block_step(carry_all, block_idx):
            carried, final_state = carry_all
            pieces = tuple((lax.dynamic_index_in_dim(part_arr, block_idx, axis=1, keepdims=False) for part_arr in ready))
            block_out, carried = advance(carried, *pieces)
            final_state = jnp.where(block_idx == block_total - 1, carried, final_state)
            return ((carried, final_state), block_out)
        (carried, final_state), stacked = lax.scan(block_step, (initial, jnp.zeros_like(initial)), jnp.arange(blocks_per, dtype=jnp.int32))
        token_out = jnp.transpose(stacked, (0, 2, 1, 3)).reshape(TAIL_POSITIONS, OUTPUT_CHANNELS, DV)
        live_mask = jnp.arange(TAIL_POSITIONS, dtype=jnp.int32) < block_total * BLOCK
        spread = lax.optimization_barrier(jnp.mean(token_out * token_out, axis=-1, keepdims=True))
        normed = token_out * lax.rsqrt(spread + EPSILON) * norm_gain * jax.nn.silu(gate_part.astype(jnp.float32))
        normed = jnp.where(live_mask[:, None, None], normed, 0.0).astype(jnp.bfloat16)
        grouped = normed.reshape(TAIL_POSITIONS, N_HEAD, group_width).astype(jnp.float32)
        partial_sums = jnp.einsum('tgc,gcd->gtd', grouped, weight_groups)
        rounded = lax.optimization_barrier(partial_sums.astype(jnp.bfloat16))
        return (lax.optimization_barrier(jnp.sum(rounded.astype(jnp.float32), axis=0)).astype(jnp.bfloat16), final_state)
    layer_rows, finals = lax.map(serve, (queries.reshape(REQS, TAIL_POSITIONS, HK, DK), key_rows.reshape(REQS, TAIL_POSITIONS, HK, DK), values.reshape(REQS, TAIL_POSITIONS, OUTPUT_CHANNELS, DV), gate_input.reshape(REQS, TAIL_POSITIONS, OUTPUT_CHANNELS, DV), write_rate.reshape(REQS, TAIL_POSITIONS, OUTPUT_CHANNELS), log_decay.reshape(REQS, TAIL_POSITIONS, OUTPUT_CHANNELS), slot_index, suffix_blocks.astype(jnp.int32)))
    layer_out = layer_rows.reshape(TOKENS, D)
    targets = (cache_owner * REQ_DEV + new_slot).astype(jnp.int32)
    new_cache = jnp.zeros((NEW_SLOTS, OUTPUT_CHANNELS, DK, DV), jnp.float32).at[targets].set(finals)
    return (layer_out, new_cache)
```

```python
import functools

import jax
import jax.numpy as jnp
from jax import lax
from jax.experimental import pallas as pl
from jax.experimental.pallas import tpu as pltpu
from jax.sharding import PartitionSpec as P

BLOCK = 64
TAIL_POSITIONS = 128
WIDTH = 128
BASE = 16
EPSILON = 1e-06
HIGHEST = lax.Precision.HIGHEST
BF16 = jnp.bfloat16
F32 = jnp.float32
VMEM_LIMIT = 56 * 1024 * 1024


def iota(shape, dim):
    return lax.broadcasted_iota(jnp.int32, shape, dim)


def dot(left, right, dims=((1,), (0,))):
    return lax.dot_general(left, right, (dims, ((), ())), preferred_element_type=F32)


def params(**kwargs):
    return pltpu.CompilerParams(vmem_limit_bytes=VMEM_LIMIT, **kwargs)


def pick_kernel(per_step, slot_ref, cache_ref, out_ref):
    step = pl.program_id(0)
    for i in range(per_step):
        out_ref[i] = cache_ref[slot_ref[step * per_step + i]].astype(BF16)


def pick_states(wanted, cache_states, chunk, heads):
    slots = cache_states.shape[0]
    count = wanted.shape[0]
    per_step = min(8, count)
    return pl.pallas_call(
        functools.partial(pick_kernel, per_step),
        out_shape=jax.ShapeDtypeStruct((count, heads, WIDTH, WIDTH), BF16),
        grid_spec=pltpu.PrefetchScalarGridSpec(
            num_scalar_prefetch=1,
            grid=(count // per_step,),
            in_specs=[
                pl.BlockSpec((slots, heads, WIDTH, WIDTH), lambda s, _: (0, chunk, 0, 0))
            ],
            out_specs=pl.BlockSpec(
                (per_step, heads, WIDTH, WIDTH), lambda s, _: (s, 0, 0, 0)
            ),
        ),
        compiler_params=params(),
        cost_estimate=pl.CostEstimate(
            flops=0, bytes_accessed=6 * count * heads * WIDTH * WIDTH, transcendentals=0
        ),
        name="pick_states",
    )(wanted, cache_states)


def unit_rows(vectors):
    vectors = vectors.astype(F32)
    return vectors * lax.rsqrt(
        jnp.sum(vectors * vectors, axis=-1, keepdims=True) + EPSILON
    )


def unit_lower_inverse(systems):
    count = len(systems)
    shape = (TAIL_POSITIONS, TAIL_POSITIONS)
    row, col = iota(shape, 0), iota(shape, 1)
    parts = TAIL_POSITIONS // BASE
    diagonal = (row // BASE) == (col // BASE)
    packed = []
    for system in systems:
        inner = jnp.where(diagonal, system, 0.0)
        total = inner[:BASE]
        for part in range(1, parts):
            total = total + inner[part * BASE : (part + 1) * BASE]
        packed.append(total)
    short = (BASE, TAIL_POSITIONS)
    lane = iota(short, 1)
    first = jnp.where(iota(short, 0) == lane % BASE, 1.0, 0.0)
    solved = [first] * count
    for step in range(BASE - 1):
        index = (lane // BASE) * BASE + step
        for i in range(count):
            factor = jnp.take_along_axis(packed[i], index, axis=1)
            solved[i] = solved[i] - factor * solved[i][step : step + 1]
    inverses = [
        jnp.where(diagonal, jnp.concatenate([x] * parts, axis=0), 0.0) for x in solved
    ]
    size = BASE
    while size < TAIL_POSITIONS:
        if size * 2 < TAIL_POSITIONS:
            below = ((row // (2 * size)) == (col // (2 * size))) & (
                (row // size) != (col // size)
            )
            short_inv = [x.astype(BF16) for x in inverses]
            moved = [
                dot(jnp.where(below, system, 0.0).astype(BF16), x).astype(BF16)
                for system, x in zip(systems, short_inv)
            ]
            inverses = [
                x - dot(s, m) for x, s, m in zip(inverses, short_inv, moved)
            ]
        else:
            short_inv = [x.astype(BF16) for x in inverses]
            moved = [
                dot(system[size:, :size].astype(BF16), x[:size, :size]).astype(BF16)
                for system, x in zip(systems, short_inv)
            ]
            corner = [dot(x[size:, size:], m) for x, m in zip(short_inv, moved)]
            inverses = [
                jnp.concatenate(
                    [x[:size], jnp.concatenate([-c, x[size:, size:]], axis=1)], axis=0
                )
                for x, c in zip(inverses, corner)
            ]
        size *= 2
    return inverses


def prep_kernel(per_step, blocks_ref, q_ref, k_ref, v_ref, rows_ref, maps_ref, own_ref):
    step = pl.program_id(0)
    tokens = TAIL_POSITIONS
    square = (tokens, tokens)
    row, col = iota(square, 0), iota(square, 1)
    upto = jnp.where(row <= col, 1.0, 0.0)
    within = row >= col
    strict = row > col
    scale = WIDTH ** (-0.5)

    masked = []
    for r in range(per_step):
        live = iota((4, tokens), 1) < blocks_ref[step * per_step + r] * BLOCK
        masked.append(jnp.where(live, rows_ref[0, :, r * tokens : (r + 1) * tokens], 0.0))
    masked = jnp.concatenate(masked, axis=0)
    running = lax.dot_general(
        masked, upto, (((1,), (0,)), ((), ())), precision=HIGHEST, preferred_element_type=F32
    )
    tall = jnp.transpose(jnp.concatenate([masked, running], axis=0))

    keys, queries, systems, fades, scores = [], [], [], [], []
    for r in range(per_step):
        span = pl.ds(r * tokens, tokens)
        k = unit_rows(k_ref[span, :]).astype(BF16)
        q = (unit_rows(q_ref[span, :]) * scale).astype(BF16)
        keys.append(k)
        queries.append(q)
        pair = dot(jnp.concatenate([k, q], axis=0), k, ((1,), (1,)))
        for h in range(2):
            at = r * 4 + 2 + h
            run_row = running[at : at + 1]
            run_col = tall[:, per_step * 4 + at : per_step * 4 + at + 1]
            rate_col = tall[:, r * 4 + h : r * 4 + h + 1]
            fade = jnp.exp(jnp.where(within, run_col - run_row, -1e30))
            systems.append(jnp.where(strict, rate_col * pair[:tokens] * fade, 0.0))
            scores.append((pair[tokens:] * fade).astype(BF16))
    inverses = unit_lower_inverse(systems)
    solved = []
    for r in range(per_step):
        key_wide = keys[r].astype(F32)
        for h in range(2):
            i = r * 2 + h
            at = r * 4 + 2 + h
            grow_col = jnp.exp(tall[:, per_step * 4 + at : per_step * 4 + at + 1])
            rate_row = masked[r * 4 + h : r * 4 + h + 1]
            left = (inverses[i] * rate_row).astype(BF16)
            right = jnp.concatenate(
                [
                    v_ref[pl.ds(r * tokens, tokens), h * WIDTH : (h + 1) * WIDTH],
                    (key_wide * grow_col).astype(BF16),
                ],
                axis=1,
            )
            solved.append(dot(left, right).astype(BF16))
    for r in range(per_step):
        key_turned = jnp.transpose(keys[r].astype(F32))
        query_wide = queries[r].astype(F32)
        for h in range(2):
            i = r * 2 + h
            at = r * 4 + 2 + h
            run_row = running[at : at + 1]
            end = run_row[:, tokens - 1 : tokens]
            grow_col = jnp.exp(tall[:, per_step * 4 + at : per_step * 4 + at + 1])
            ending = (key_turned * jnp.exp(end - run_row)).astype(BF16)
            both = dot(jnp.concatenate([scores[i], ending], axis=0), solved[i])
            own_ref[r, h] = both[:, :WIDTH].astype(BF16)
            kept = jnp.where(row == col, jnp.exp(end), 0.0)
            maps_ref[r, h, :tokens] = (query_wide * grow_col - both[:tokens, WIDTH:]).astype(BF16)
            maps_ref[r, h, tokens:] = (kept - both[tokens:, WIDTH:]).astype(BF16)


def prepare(blocks, queries, keys, values, rows, chunk):
    requests = blocks.shape[0]
    per_step = 4
    span = per_step * TAIL_POSITIONS
    tall = (requests, 2, TAIL_POSITIONS + WIDTH, WIDTH)
    block = pl.BlockSpec((per_step,) + tall[1:], lambda s, _: (s, 0, 0, 0))
    return pl.pallas_call(
        functools.partial(prep_kernel, per_step),
        out_shape=(jax.ShapeDtypeStruct(tall, BF16), jax.ShapeDtypeStruct(tall, BF16)),
        grid_spec=pltpu.PrefetchScalarGridSpec(
            num_scalar_prefetch=1,
            grid=(requests // per_step,),
            in_specs=[
                pl.BlockSpec((span, WIDTH), lambda s, _: (s, chunk)),
                pl.BlockSpec((span, WIDTH), lambda s, _: (s, chunk)),
                pl.BlockSpec((span, 2 * WIDTH), lambda s, _: (s, chunk)),
                pl.BlockSpec((1, 4, span), lambda s, _: (chunk, 0, s)),
            ],
            out_specs=(block, block),
        ),
        compiler_params=params(),
        cost_estimate=pl.CostEstimate(
            flops=requests * 2 * 24 * 2 * 128**3, bytes_accessed=24 << 20, transcendentals=0
        ),
        name="prepare",
    )(blocks, queries, keys, values, rows)


def advance_kernel(
    per_step, owner_ref, blocks_ref, state_ref, maps_ref, own_ref, gate_ref, gain_ref, normed_ref, final_ref
):
    step = pl.program_id(0)
    tokens = TAIL_POSITIONS
    gain = gain_ref[...]
    for r in range(per_step):
        request = step * per_step + r
        owner = owner_ref[request]
        live = iota((tokens, WIDTH), 0) < blocks_ref[request] * BLOCK
        for h in range(2):
            both = dot(maps_ref[r, h], state_ref[owner, h]) + own_ref[r, h].astype(F32)
            final_ref[owner, h] = both[tokens:].astype(BF16)
            core = both[:tokens]
            gate = gate_ref[pl.ds(r * tokens, tokens), h * WIDTH : (h + 1) * WIDTH].astype(F32)
            spread = jnp.mean(core * core, axis=-1, keepdims=True)
            normed = core * lax.rsqrt(spread + EPSILON) * gain * (gate / (1.0 + jnp.exp(-gate)))
            normed_ref[pl.ds(r * tokens, tokens), h * WIDTH : (h + 1) * WIDTH] = jnp.where(
                live, normed, 0.0
            ).astype(BF16)


def advance(owners, blocks, states, maps, own, gates, gain, chunk):
    requests = blocks.shape[0]
    per_step = 4
    span = per_step * TAIL_POSITIONS
    tall = (per_step, 2, TAIL_POSITIONS + WIDTH, WIDTH)
    whole = pl.BlockSpec(states.shape, lambda s, *_: (0, 0, 0, 0))
    return pl.pallas_call(
        functools.partial(advance_kernel, per_step),
        out_shape=(
            jax.ShapeDtypeStruct((requests * TAIL_POSITIONS, 2 * WIDTH), BF16),
            jax.ShapeDtypeStruct(states.shape, BF16),
        ),
        grid_spec=pltpu.PrefetchScalarGridSpec(
            num_scalar_prefetch=2,
            grid=(requests // per_step,),
            in_specs=[
                whole,
                pl.BlockSpec(tall, lambda s, *_: (s, 0, 0, 0)),
                pl.BlockSpec(tall, lambda s, *_: (s, 0, 0, 0)),
                pl.BlockSpec((span, 2 * WIDTH), lambda s, *_: (s, chunk)),
                pl.BlockSpec((1, WIDTH), lambda s, *_: (0, 0)),
            ],
            out_specs=(
                pl.BlockSpec((span, 2 * WIDTH), lambda s, *_: (s, 0)),
                whole,
            ),
        ),
        compiler_params=params(),
        cost_estimate=pl.CostEstimate(
            flops=requests * 2 * 4 * 128**3, bytes_accessed=16 << 20, transcendentals=0
        ),
        name="advance",
    )(owners, blocks, states, maps, own, gates, gain)


def place_kernel(per_step, source_ref, arrived_ref, *refs):
    out_ref = refs[-1]
    step = pl.program_id(0)
    for i in range(per_step):
        out_ref[i] = arrived_ref[source_ref[step * per_step + i]].astype(F32)


def place(source, arrived, earlier, chunk, heads_all):
    slots = source.shape[0]
    heads = arrived.shape[1]
    per_step = 4
    operands = [source, arrived]
    in_specs = [pl.BlockSpec(arrived.shape, lambda s, _: (0, 0, 0, 0))]
    aliases = {}
    if earlier is not None:
        operands.append(earlier)
        in_specs.append(pl.BlockSpec(memory_space=pl.ANY))
        aliases = {2: 0}
    return pl.pallas_call(
        functools.partial(place_kernel, per_step),
        out_shape=jax.ShapeDtypeStruct((slots, heads_all, WIDTH, WIDTH), F32),
        grid_spec=pltpu.PrefetchScalarGridSpec(
            num_scalar_prefetch=1,
            grid=(slots // per_step,),
            in_specs=in_specs,
            out_specs=pl.BlockSpec(
                (per_step, heads, WIDTH, WIDTH), lambda s, _: (s, chunk, 0, 0)
            ),
        ),
        input_output_aliases=aliases,
        compiler_params=params(),
        cost_estimate=pl.CostEstimate(flops=0, bytes_accessed=5 << 20, transcendentals=0),
        name="place",
    )(*operands)


def project_kernel(groups, *refs):
    *arrived, weight_ref, out_ref = refs
    chunks = len(arrived)
    width = arrived[0].shape[2]
    total = None
    for group in range(groups):
        for chunk in range(chunks):
            first = (group * chunks + chunk) * width
            term = dot(arrived[chunk][group], weight_ref[pl.ds(first, width), :])
            total = term if total is None else total + term
    out_ref[...] = total.astype(BF16)


def project(arrived, weight):
    groups, rows, width = arrived[0].shape
    model = weight.shape[1]
    tile = 256
    return pl.pallas_call(
        functools.partial(project_kernel, groups),
        out_shape=jax.ShapeDtypeStruct((rows, model), BF16),
        grid=(model // tile,),
        in_specs=[
            pl.BlockSpec(a.shape, lambda n: (0, 0, 0), pipeline_mode=pl.Buffered(1))
            for a in arrived
        ]
        + [pl.BlockSpec((weight.shape[0], tile), lambda n: (0, n))],
        out_specs=pl.BlockSpec((rows, tile), lambda n: (0, n)),
        compiler_params=params(),
        cost_estimate=pl.CostEstimate(
            flops=2 * rows * weight.shape[0] * model, bytes_accessed=16 << 20, transcendentals=0
        ),
        name="project",
    )(*arrived, weight)


def local(
    queries,
    key_rows,
    values,
    gate_input,
    write_rate,
    log_decay,
    norm_gain,
    out_weight,
    cache_states,
    cache_owner,
    cache_slot,
    suffix_blocks,
    new_slot,
):
    owner_count = lax.axis_size("req")
    groups = lax.axis_size("head")
    device = lax.axis_index("req")
    tokens = queries.shape[0]
    requests = tokens // TAIL_POSITIONS
    heads_all = values.shape[1]
    chunks = queries.shape[1]
    heads = heads_all // chunks

    naming = cache_owner.reshape(owner_count, requests) == device
    wanted = jnp.sum(jnp.where(naming, cache_slot.reshape(owner_count, requests), 0), axis=1)
    picked = [pick_states(wanted, cache_states, c, heads) for c in range(chunks)]
    arrived = [
        lax.all_to_all(p, "req", split_axis=0, concat_axis=0, tiled=True) for p in picked
    ]
    weight = lax.all_gather(out_weight, "head", axis=0, tiled=True)

    my_owner = lax.dynamic_slice_in_dim(cache_owner, device * requests, requests)
    my_blocks = lax.dynamic_slice_in_dim(suffix_blocks, device * requests, requests)
    slot_ids = jnp.arange(requests, dtype=jnp.int32)
    claimed = naming[None] & (
        new_slot.reshape(owner_count, requests)[None] == slot_ids[:, None, None]
    )
    device_ids = jnp.arange(owner_count, dtype=jnp.int32)[None, :, None]
    source = jnp.sum(jnp.where(claimed, device_ids, 0), axis=(1, 2))

    query_flat = queries.reshape(tokens, -1)
    key_flat = key_rows.reshape(tokens, -1)
    value_flat = values.reshape(tokens, -1)
    gate_flat = gate_input.reshape(tokens, -1)
    rows = jnp.concatenate(
        [
            write_rate.T.reshape(chunks, heads, tokens),
            log_decay.T.reshape(chunks, heads, tokens),
        ],
        axis=1,
    )
    gain = norm_gain.reshape(1, -1)

    leaving, shares = [], []
    ready = [
        prepare(my_blocks, query_flat, key_flat, value_flat, rows, c) for c in range(chunks)
    ]
    for c in range(chunks):
        normed, final = advance(my_owner, my_blocks, arrived[c], *ready[c], gate_flat, gain, c)
        leaving.append(lax.all_to_all(final, "req", split_axis=0, concat_axis=0, tiled=True))
        shares.append(
            lax.all_to_all(
                normed.reshape(groups, tokens // groups, heads * WIDTH),
                "head",
                split_axis=0,
                concat_axis=0,
                tiled=True,
            )
        )
    layer_out = project(shares, weight)
    new_cache = None
    for c in range(chunks):
        new_cache = place(source, leaving[c], new_cache, c, heads_all)
    return (layer_out, new_cache)


def solution(mesh):
    return jax.shard_map(
        local,
        mesh=mesh,
        in_specs=(
            P("req", "head", None),
            P("req", "head", None),
            P("req", "head", None),
            P("req", "head", None),
            P("req", "head"),
            P("req", "head"),
            P(),
            P("head", None),
            P("req", "head", None, None),
            P(),
            P(),
            P(),
            P(),
        ),
        out_specs=(P(("req", "head"), None), P("req", "head", None, None)),
        check_vma=False,
    )
```

```python
import functools

import jax
import jax.numpy as jnp
from jax import lax
from jax.experimental import pallas as pl
from jax.experimental.pallas import tpu as pltpu
from jax.sharding import PartitionSpec as P

BLOCK = 64
TAIL_POSITIONS = 128
WIDTH = 128
BASE = 8
EPSILON = 1e-06
HIGHEST = lax.Precision.HIGHEST
BF16 = jnp.bfloat16
F32 = jnp.float32


def iota(shape, dim):
    return lax.broadcasted_iota(jnp.int32, shape, dim)


def dot(left, right, dims=((1,), (0,))):
    return lax.dot_general(left, right, (dims, ((), ())), preferred_element_type=F32)


def params():
    return pltpu.CompilerParams(vmem_limit_bytes=(64 << 20) - (1 << 18))


def pick_kernel(wanted_ref, cache_ref, out_ref, wide, short, in_sems, out_sems):
    slots, count = cache_ref.shape[0], out_ref.shape[0]
    loads = [
        pltpu.make_async_copy(cache_ref.at[i], wide.at[i], in_sems.at[i]) for i in range(slots)
    ]
    for load in loads:
        load.start()
    for i, load in enumerate(loads):
        load.wait()
        short[i] = wide[i].astype(BF16)
    stores = [
        pltpu.make_async_copy(short.at[wanted_ref[i]], out_ref.at[i], out_sems.at[i])
        for i in range(count)
    ]
    for store in stores:
        store.start()
    for store in stores:
        store.wait()


def pick_states(wanted, cache_states):
    count = wanted.shape[0]
    one = cache_states.shape[1:]
    return pl.pallas_call(
        pick_kernel,
        out_shape=jax.ShapeDtypeStruct((count,) + one, BF16),
        grid_spec=pltpu.PrefetchScalarGridSpec(
            num_scalar_prefetch=1,
            grid=(1,),
            in_specs=[pl.BlockSpec(memory_space=pl.ANY)],
            out_specs=pl.BlockSpec(memory_space=pl.ANY),
            scratch_shapes=[
                pltpu.VMEM(cache_states.shape, F32),
                pltpu.VMEM(cache_states.shape, BF16),
                pltpu.SemaphoreType.DMA((cache_states.shape[0],)),
                pltpu.SemaphoreType.DMA((count,)),
            ],
        ),
        compiler_params=params(),
        cost_estimate=pl.CostEstimate(flops=0, bytes_accessed=6 << 20, transcendentals=0),
        name="pick_states",
    )(wanted, cache_states)


def unit_rows(vectors):
    vectors = vectors.astype(F32)
    return vectors * lax.rsqrt(
        jnp.sum(vectors * vectors, axis=-1, keepdims=True) + EPSILON
    )


def unit_lower_inverse(systems):
    count = len(systems)
    shape = (TAIL_POSITIONS, TAIL_POSITIONS)
    row, col = iota(shape, 0), iota(shape, 1)
    parts = TAIL_POSITIONS // BASE
    diagonal = (row // BASE) == (col // BASE)
    packed = []
    for system in systems:
        inner = jnp.where(diagonal, system, 0.0)
        total = inner[:BASE]
        for part in range(1, parts):
            total = total + inner[part * BASE : (part + 1) * BASE]
        packed.append(total)
    short = (BASE, TAIL_POSITIONS)
    lane = iota(short, 1)
    first = jnp.where(iota(short, 0) == lane % BASE, 1.0, 0.0)
    solved = [first] * count
    for step in range(BASE - 1):
        index = (lane // BASE) * BASE + step
        for i in range(count):
            factor = jnp.take_along_axis(packed[i], index, axis=1)
            solved[i] = solved[i] - factor * solved[i][step : step + 1]
    inverses = [
        jnp.where(diagonal, jnp.concatenate([x] * parts, axis=0), 0.0) for x in solved
    ]
    size = BASE
    while size < TAIL_POSITIONS:
        if size * 2 < TAIL_POSITIONS:
            below = ((row // (2 * size)) == (col // (2 * size))) & (
                (row // size) != (col // size)
            )
            short_inv = [x.astype(BF16) for x in inverses]
            moved = [
                dot(jnp.where(below, system, 0.0).astype(BF16), x).astype(BF16)
                for system, x in zip(systems, short_inv)
            ]
            inverses = [
                x - dot(s, m) for x, s, m in zip(inverses, short_inv, moved)
            ]
        else:
            short_inv = [x.astype(BF16) for x in inverses]
            moved = [
                dot(system[size:, :size].astype(BF16), x[:size, :size]).astype(BF16)
                for system, x in zip(systems, short_inv)
            ]
            corner = [dot(x[size:, size:], m) for x, m in zip(short_inv, moved)]
            inverses = [
                jnp.concatenate(
                    [x[:size], jnp.concatenate([-c, x[size:, size:]], axis=1)], axis=0
                )
                for x, c in zip(inverses, corner)
            ]
        size *= 2
    return inverses


def prep_kernel(per_step, blocks_ref, q_ref, k_ref, v_ref, rows_ref, core_ref, final_ref):
    step = pl.program_id(0)
    tokens = TAIL_POSITIONS
    square = (tokens, tokens)
    row, col = iota(square, 0), iota(square, 1)
    upto = jnp.where(row <= col, 1.0, 0.0)
    within = row >= col
    strict = row > col
    scale = WIDTH ** (-0.5)

    masked = []
    for r in range(per_step):
        live = iota((4, tokens), 1) < blocks_ref[step * per_step + r] * BLOCK
        masked.append(jnp.where(live, rows_ref[0, :, r * tokens : (r + 1) * tokens], 0.0))
    masked = jnp.concatenate(masked, axis=0)
    running = lax.dot_general(
        masked, upto, (((1,), (0,)), ((), ())), precision=HIGHEST, preferred_element_type=F32
    )
    tall = jnp.transpose(jnp.concatenate([masked, running], axis=0))

    keys, queries, systems, fades, scores = [], [], [], [], []
    for r in range(per_step):
        span = pl.ds(r * tokens, tokens)
        k = unit_rows(k_ref[span, :]).astype(BF16)
        q = (unit_rows(q_ref[span, :]) * scale).astype(BF16)
        keys.append(k)
        queries.append(q)
        pair = dot(jnp.concatenate([k, q], axis=0), k, ((1,), (1,)))
        for h in range(2):
            at = r * 4 + 2 + h
            run_row = running[at : at + 1]
            run_col = tall[:, per_step * 4 + at : per_step * 4 + at + 1]
            rate_col = tall[:, r * 4 + h : r * 4 + h + 1]
            fade = jnp.exp(jnp.where(within, run_col - run_row, -1e30))
            systems.append(jnp.where(strict, rate_col * pair[:tokens] * fade, 0.0))
            scores.append((pair[tokens:] * fade).astype(BF16))
    inverses = unit_lower_inverse(systems)
    solved = []
    for r in range(per_step):
        key_wide = keys[r].astype(F32)
        for h in range(2):
            i = r * 2 + h
            at = r * 4 + 2 + h
            grow_col = jnp.exp(tall[:, per_step * 4 + at : per_step * 4 + at + 1])
            rate_row = masked[r * 4 + h : r * 4 + h + 1]
            left = (inverses[i] * rate_row).astype(BF16)
            right = jnp.concatenate(
                [
                    v_ref[pl.ds(r * tokens, tokens), h * WIDTH : (h + 1) * WIDTH],
                    (key_wide * grow_col).astype(BF16),
                ],
                axis=1,
            )
            solved.append(dot(left, right).astype(BF16))
    for r in range(per_step):
        key_turned = jnp.transpose(keys[r].astype(F32))
        query_wide = queries[r].astype(F32)
        for h in range(2):
            i = r * 2 + h
            at = r * 4 + 2 + h
            run_row = running[at : at + 1]
            end = run_row[:, tokens - 1 : tokens]
            grow_col = jnp.exp(tall[:, per_step * 4 + at : per_step * 4 + at + 1])
            ending = (key_turned * jnp.exp(end - run_row)).astype(BF16)
            both = dot(jnp.concatenate([scores[i], ending], axis=0), solved[i])
            kept = jnp.where(row == col, jnp.exp(end), 0.0)
            core_ref[r, h, :WIDTH] = (query_wide * grow_col - both[:tokens, WIDTH:]).astype(BF16)
            core_ref[r, h, WIDTH:] = both[:tokens, :WIDTH].astype(BF16)
            final_ref[r, h, :WIDTH] = (kept - both[tokens:, WIDTH:]).astype(BF16)
            final_ref[r, h, WIDTH:] = both[tokens:, :WIDTH].astype(BF16)


def prepare(blocks, queries, keys, values, rows):
    requests = blocks.shape[0]
    chunks = rows.shape[0]
    per_step = 8 if requests % 8 == 0 else 4
    span = per_step * TAIL_POSITIONS
    tall = (requests, 2 * chunks, 2 * WIDTH, WIDTH)
    block = pl.BlockSpec((per_step, 2) + tall[2:], lambda s, c, _: (s, c, 0, 0))
    return pl.pallas_call(
        functools.partial(prep_kernel, per_step),
        out_shape=(jax.ShapeDtypeStruct(tall, BF16), jax.ShapeDtypeStruct(tall, BF16)),
        grid_spec=pltpu.PrefetchScalarGridSpec(
            num_scalar_prefetch=1,
            grid=(requests // per_step, chunks),
            in_specs=[
                pl.BlockSpec((span, WIDTH), lambda s, c, _: (s, c)),
                pl.BlockSpec((span, WIDTH), lambda s, c, _: (s, c)),
                pl.BlockSpec((span, 2 * WIDTH), lambda s, c, _: (s, c)),
                pl.BlockSpec((1, 4, span), lambda s, c, _: (c, 0, s)),
            ],
            out_specs=(block, block),
        ),
        compiler_params=params(),
        cost_estimate=pl.CostEstimate(
            flops=requests * 4 * 24 * 2 * 128**3, bytes_accessed=24 << 20, transcendentals=0
        ),
        name="prepare",
    )(blocks, queries, keys, values, rows)


def finish_kernel(owner_ref, state_ref, maps_ref, out_ref, states, maps, finals, state_sems, map_sems, out_sems):
    requests, heads = maps_ref.shape[:2]
    loads = []
    for r in range(requests):
        pair = (
            pltpu.make_async_copy(state_ref.at[owner_ref[r]], states.at[r], state_sems.at[r]),
            pltpu.make_async_copy(maps_ref.at[r], maps.at[r], map_sems.at[r]),
        )
        for load in pair:
            load.start()
        loads.append(pair)
    stores = []
    for r in range(requests):
        for load in loads[r]:
            load.wait()
        for h in range(heads):
            moved = dot(maps[r, h, :WIDTH], states[r, h])
            finals[r, h] = (moved + maps[r, h, WIDTH:].astype(F32)).astype(BF16)
        store = pltpu.make_async_copy(finals.at[r], out_ref.at[owner_ref[r]], out_sems.at[r])
        store.start()
        stores.append(store)
    for store in stores:
        store.wait()


def finish(owners, states, maps):
    requests = maps.shape[0]
    one = states.shape[1:]
    return pl.pallas_call(
        finish_kernel,
        out_shape=jax.ShapeDtypeStruct(states.shape, BF16),
        grid_spec=pltpu.PrefetchScalarGridSpec(
            num_scalar_prefetch=1,
            grid=(1,),
            in_specs=[pl.BlockSpec(memory_space=pl.ANY)] * 2,
            out_specs=pl.BlockSpec(memory_space=pl.ANY),
            scratch_shapes=[
                pltpu.VMEM((requests,) + one, BF16),
                pltpu.VMEM(maps.shape, BF16),
                pltpu.VMEM((requests,) + one, BF16),
                pltpu.SemaphoreType.DMA((requests,)),
                pltpu.SemaphoreType.DMA((requests,)),
                pltpu.SemaphoreType.DMA((requests,)),
            ],
        ),
        compiler_params=params(),
        cost_estimate=pl.CostEstimate(
            flops=requests * 4 * 2 * 128**3, bytes_accessed=13 << 20, transcendentals=0
        ),
        name="finish",
    )(owners, states, maps)


def block_at(step, group_ref, group_steps, groups, shifts):
    shift = shifts[-1]
    for i in range(len(shifts) - 1):
        shift = jnp.where(step // group_steps == i, shifts[i], shift)
    return ((group_ref[0] + shift) % groups) * group_steps + step % group_steps


def emit_kernel(per_step, group_steps, groups, shifts, owner_ref, blocks_ref, group_ref, *refs):
    state_refs = refs[:per_step]
    maps_ref, gate_ref, gain_ref = refs[per_step : per_step + 3]
    out_refs = refs[per_step + 3 :]
    step = pl.program_id(0)
    first = block_at(step, group_ref, group_steps, groups, shifts) * per_step
    tokens = TAIL_POSITIONS
    heads = maps_ref.shape[1]
    gain = gain_ref[...]
    rows = []
    for r in range(per_step):
        live = iota((tokens, WIDTH), 0) < blocks_ref[first + r] * BLOCK
        parts = []
        for h in range(heads):
            core = dot(maps_ref[r, h, :WIDTH], state_refs[r][0, h]) + maps_ref[r, h, WIDTH:].astype(F32)
            gate = gate_ref[pl.ds(r * tokens, tokens), h * WIDTH : (h + 1) * WIDTH].astype(F32)
            spread = jnp.mean(core * core, axis=-1, keepdims=True)
            normed = core * lax.rsqrt(spread + EPSILON) * gain * (gate / (1.0 + jnp.exp(-gate)))
            parts.append(jnp.where(live, normed, 0.0).astype(BF16))
        rows.append(jnp.concatenate(parts, axis=1))
    for i in range(len(shifts)):

        @pl.when(step // group_steps == i)
        def _(i=i):
            for r in range(per_step):
                out_refs[i][pl.ds(r * tokens, tokens), :] = rows[r]


def emit(owners, blocks, group, groups, shifts, states, maps, gates, gain):
    requests = blocks.shape[0]
    share = requests // groups
    per_step = 6 if share % 6 == 0 else 1
    group_steps = share // per_step
    span = per_step * TAIL_POSITIONS
    heads = maps.shape[1]

    def at(step, group_ref):
        return block_at(step, group_ref, group_steps, groups, shifts)

    def state_spec(r):
        return pl.BlockSpec(
            (1,) + states.shape[1:], lambda s, o, b, g: (o[at(s, g) * per_step + r], 0, 0, 0)
        )

    def out_spec(i):
        return pl.BlockSpec(
            (span, heads * WIDTH),
            lambda s, o, b, g: (jnp.clip(s - i * group_steps, 0, group_steps - 1), 0),
        )

    return pl.pallas_call(
        functools.partial(emit_kernel, per_step, group_steps, groups, shifts),
        out_shape=[
            jax.ShapeDtypeStruct((share * TAIL_POSITIONS, heads * WIDTH), BF16)
            for _ in shifts
        ],
        grid_spec=pltpu.PrefetchScalarGridSpec(
            num_scalar_prefetch=3,
            grid=(len(shifts) * group_steps,),
            in_specs=[state_spec(r) for r in range(per_step)]
            + [
                pl.BlockSpec((per_step,) + maps.shape[1:], lambda s, o, b, g: (at(s, g), 0, 0, 0)),
                pl.BlockSpec((span, heads * WIDTH), lambda s, o, b, g: (at(s, g), 0)),
                pl.BlockSpec((1, WIDTH), lambda s, o, b, g: (0, 0)),
            ],
            out_specs=[out_spec(i) for i in range(len(shifts))],
        ),
        compiler_params=params(),
        cost_estimate=pl.CostEstimate(
            flops=requests * 4 * 2 * 128**3, bytes_accessed=16 << 20, transcendentals=0
        ),
        name="emit",
    )(owners, blocks, group, *([states] * per_step), maps, gates, gain)


def place_kernel(source_ref, arrived_ref, out_ref, short, wide, in_sems, out_sems):
    slots = out_ref.shape[0]
    loads = [
        pltpu.make_async_copy(arrived_ref.at[source_ref[i]], short.at[i], in_sems.at[i])
        for i in range(slots)
    ]
    for load in loads:
        load.start()
    stores = []
    for i in range(slots):
        loads[i].wait()
        wide[i] = short[i].astype(F32)
        store = pltpu.make_async_copy(wide.at[i], out_ref.at[i], out_sems.at[i])
        store.start()
        stores.append(store)
    for store in stores:
        store.wait()


def place(source, arrived):
    slots = source.shape[0]
    shape = (slots,) + arrived.shape[1:]
    return pl.pallas_call(
        place_kernel,
        out_shape=jax.ShapeDtypeStruct(shape, F32),
        grid_spec=pltpu.PrefetchScalarGridSpec(
            num_scalar_prefetch=1,
            grid=(1,),
            in_specs=[pl.BlockSpec(memory_space=pl.ANY)],
            out_specs=pl.BlockSpec(memory_space=pl.ANY),
            scratch_shapes=[
                pltpu.VMEM(shape, BF16),
                pltpu.VMEM(shape, F32),
                pltpu.SemaphoreType.DMA((slots,)),
                pltpu.SemaphoreType.DMA((slots,)),
            ],
        ),
        compiler_params=params(),
        cost_estimate=pl.CostEstimate(flops=0, bytes_accessed=10 << 20, transcendentals=0),
        name="place",
    )(source, arrived)


def project_kernel(count, half, place_ref, *refs):
    shares, nears, fars = (refs[i * count : (i + 1) * count] for i in range(3))
    out_ref = refs[-1]
    total = refs[-2][...].astype(F32) if len(refs) > 1 + 3 * count else None
    near_at = pl.multiple_of(place_ref[0] * half, half)
    far_at = pl.multiple_of((1 - place_ref[0]) * half, half)
    for share, near, far in zip(shares, nears, fars):
        for weight, at in ((near, near_at), (far, far_at)):
            term = dot(share[:, pl.ds(at, half)], weight[...])
            total = term if total is None else total + term
    out_ref[...] = total.astype(BF16)


def project(core, shares, nears, fars, earlier):
    rows, width = shares[0].shape
    half = width // 2
    model = nears[0].shape[1]
    tile = min(512, model)

    def weight_spec(weight, far):
        if weight.shape[0] == half:
            return pl.BlockSpec((half, tile), lambda n, _: (0, n))
        return pl.BlockSpec((half, tile), lambda n, c: ((1 - c[0]) if far else c[0], n))

    out_spec = pl.BlockSpec((rows, tile), lambda n, _: (0, n))
    more = [] if earlier is None else [earlier]
    return pl.pallas_call(
        functools.partial(project_kernel, len(shares), half),
        out_shape=jax.ShapeDtypeStruct((rows, model), BF16),
        grid_spec=pltpu.PrefetchScalarGridSpec(
            num_scalar_prefetch=1,
            grid=(model // tile,),
            in_specs=[pl.BlockSpec(a.shape, lambda n, _: (0, 0)) for a in shares]
            + [weight_spec(w, False) for w in nears]
            + [weight_spec(w, True) for w in fars]
            + [out_spec] * len(more),
            out_specs=out_spec,
        ),
        compiler_params=params(),
        cost_estimate=pl.CostEstimate(
            flops=4 * rows * len(shares) * half * model, bytes_accessed=12 << 20, transcendentals=0
        ),
        name="project",
    )(core, *shares, *nears, *fars, *more)


def local(
    queries,
    key_rows,
    values,
    gate_input,
    write_rate,
    log_decay,
    norm_gain,
    out_weight,
    cache_states,
    cache_owner,
    cache_slot,
    suffix_blocks,
    new_slot,
):
    owner_count = lax.axis_size("req")
    groups = lax.axis_size("head")
    device = lax.axis_index("req")
    tokens = queries.shape[0]
    requests = tokens // TAIL_POSITIONS
    heads_all = values.shape[1]
    chunks = queries.shape[1]
    heads = heads_all // chunks

    naming = cache_owner.reshape(owner_count, requests) == device
    wanted = jnp.sum(jnp.where(naming, cache_slot.reshape(owner_count, requests), 0), axis=1)
    picked = pick_states(wanted, cache_states)
    arrived = lax.all_to_all(picked, "req", split_axis=0, concat_axis=0, tiled=True)

    my_owner = lax.dynamic_slice_in_dim(cache_owner, device * requests, requests)
    my_blocks = lax.dynamic_slice_in_dim(suffix_blocks, device * requests, requests)
    slot_ids = jnp.arange(requests, dtype=jnp.int32)
    claimed = naming[None] & (
        new_slot.reshape(owner_count, requests)[None] == slot_ids[:, None, None]
    )
    device_ids = jnp.arange(owner_count, dtype=jnp.int32)[None, :, None]
    source = jnp.sum(jnp.where(claimed, device_ids, 0), axis=(1, 2))

    query_flat = queries.reshape(tokens, -1)
    key_flat = key_rows.reshape(tokens, -1)
    value_flat = values.reshape(tokens, -1)
    gate_flat = gate_input.reshape(tokens, -1)
    half = out_weight.shape[0] // 2
    core = device % 2
    out_weight, key_flat = lax.optimization_barrier((out_weight, key_flat))
    own_rows = lax.dynamic_slice_in_dim(out_weight, core * half, half)
    nears = [
        lax.ppermute(own_rows, "head", [(i, (i + d) % groups) for i in range(groups)])
        for d in range(1, groups)
    ]
    rows = jnp.concatenate(
        [
            write_rate.T.reshape(chunks, heads, tokens),
            log_decay.T.reshape(chunks, heads, tokens),
        ],
        axis=1,
    )
    gain = norm_gain.reshape(1, -1)

    core_maps, final_maps = prepare(my_blocks, query_flat, key_flat, value_flat, rows)
    gate_flat, my_owner, nears, arrived, final_maps = lax.optimization_barrier(
        (gate_flat, my_owner, nears, arrived, final_maps)
    )
    swap = [(i, i ^ 1) for i in range(owner_count)]
    fars = [lax.ppermute(w, "req", swap) for w in nears]
    final = finish(my_owner, arrived, final_maps)
    fars, final = lax.optimization_barrier((fars, final))
    returned = lax.all_to_all(final, "req", split_axis=0, concat_axis=0, tiled=True)
    group = lax.axis_index("head")
    shares = [None] * groups
    order = sorted(range(groups), key=lambda d: -min(d, groups - d))
    for shifts in (order[:1], order[1:]):
        made = emit(
            my_owner, my_blocks, group.reshape(1), groups, shifts, arrived, core_maps, gate_flat, gain
        )
        for d, share in zip(shifts, made):
            pairs = [(i, (i + d) % groups) for i in range(groups)]
            shares[d] = lax.ppermute(share, "head", pairs) if d else share
    early, late = order[:1] + order[-1:], order[1:-1]
    layer_out = None
    for shifts in (early, late):
        if shifts:
            weights = [[[out_weight, *part][d] for d in shifts] for part in (nears, fars)]
            taken = [[shares[d] for d in shifts], *weights]
            layer_out = project(core.reshape(1), *taken, layer_out)
    returned, layer_out = lax.optimization_barrier((returned, layer_out))
    new_cache = place(source, returned)
    return (layer_out, new_cache)


def solution(mesh):
    return jax.shard_map(
        local,
        mesh=mesh,
        in_specs=(
            P("req", "head", None),
            P("req", "head", None),
            P("req", "head", None),
            P("req", "head", None),
            P("req", "head"),
            P("req", "head"),
            P(),
            P("head", None),
            P("req", "head", None, None),
            P(),
            P(),
            P(),
            P(),
        ),
        out_specs=(P(("req", "head"), None), P("req", "head", None, None)),
        check_vma=False,
    )
```

```python
import functools

import jax
import jax.numpy as jnp
from jax import lax
from jax.experimental import pallas as pl
from jax.experimental.pallas import tpu as pltpu
from jax.sharding import PartitionSpec as P

BLOCK = 64
TAIL_POSITIONS = 128
WIDTH = 128
BASE = 8
EPSILON = 1e-06
HIGHEST = lax.Precision.HIGHEST
BF16 = jnp.bfloat16
F32 = jnp.float32


def iota(shape, dim):
    return lax.broadcasted_iota(jnp.int32, shape, dim)


def dot(left, right, dims=((1,), (0,))):
    return lax.dot_general(left, right, (dims, ((), ())), preferred_element_type=F32)


def params():
    return pltpu.CompilerParams(vmem_limit_bytes=(64 << 20) - (1 << 18))


def pick_kernel(device_ref, owner_ref, slot_ref, cache_ref, out_ref, wide, short, wanted, in_sems, out_sems):
    slots, count = cache_ref.shape[0], out_ref.shape[0]
    requests = owner_ref.shape[0] // count
    loads = [
        pltpu.make_async_copy(cache_ref.at[i], wide.at[i], in_sems.at[i]) for i in range(slots)
    ]
    for load in loads:
        load.start()
    device = device_ref[0]

    @pl.loop(0, count)
    def _(i):
        slot = 0
        for j in range(requests):
            at = i * requests + j
            slot = jnp.where(owner_ref[at] == device, slot_ref[at], slot)
        wanted[i] = slot

    for i, load in enumerate(loads):
        load.wait()
        short[i] = wide[i].astype(BF16)
    stores = [
        pltpu.make_async_copy(short.at[wanted[i]], out_ref.at[i], out_sems.at[i])
        for i in range(count)
    ]
    for store in stores:
        store.start()
    for store in stores:
        store.wait()


def pick_states(device, count, owners, slots, cache_states):
    one = cache_states.shape[1:]
    return pl.pallas_call(
        pick_kernel,
        out_shape=jax.ShapeDtypeStruct((count,) + one, BF16),
        grid_spec=pltpu.PrefetchScalarGridSpec(
            num_scalar_prefetch=3,
            grid=(1,),
            in_specs=[pl.BlockSpec(memory_space=pl.ANY)],
            out_specs=pl.BlockSpec(memory_space=pl.ANY),
            scratch_shapes=[
                pltpu.VMEM(cache_states.shape, F32),
                pltpu.VMEM(cache_states.shape, BF16),
                pltpu.SMEM((count,), jnp.int32),
                pltpu.SemaphoreType.DMA((cache_states.shape[0],)),
                pltpu.SemaphoreType.DMA((count,)),
            ],
        ),
        compiler_params=params(),
        cost_estimate=pl.CostEstimate(flops=0, bytes_accessed=6 << 20, transcendentals=0),
        name="pick_states",
    )(device, owners, slots, cache_states)


def unit_rows(vectors):
    vectors = vectors.astype(F32)
    return vectors * lax.rsqrt(
        jnp.sum(vectors * vectors, axis=-1, keepdims=True) + EPSILON
    )


def unit_lower_inverse(systems):
    count = len(systems)
    shape = (TAIL_POSITIONS, TAIL_POSITIONS)
    row, col = iota(shape, 0), iota(shape, 1)
    parts = TAIL_POSITIONS // BASE
    diagonal = (row // BASE) == (col // BASE)
    packed = []
    for system in systems:
        inner = jnp.where(diagonal, system, 0.0)
        total = inner[:BASE]
        for part in range(1, parts):
            total = total + inner[part * BASE : (part + 1) * BASE]
        packed.append(total)
    short = (BASE, TAIL_POSITIONS)
    lane = iota(short, 1)
    first = jnp.where(iota(short, 0) == lane % BASE, 1.0, 0.0)
    solved = [first] * count
    for step in range(BASE - 1):
        index = (lane // BASE) * BASE + step
        for i in range(count):
            factor = jnp.take_along_axis(packed[i], index, axis=1)
            solved[i] = solved[i] - factor * solved[i][step : step + 1]
    inverses = [
        jnp.where(diagonal, jnp.concatenate([x] * parts, axis=0), 0.0) for x in solved
    ]
    size = BASE
    while size < TAIL_POSITIONS:
        if size * 2 < TAIL_POSITIONS:
            below = ((row // (2 * size)) == (col // (2 * size))) & (
                (row // size) != (col // size)
            )
            short_inv = [x.astype(BF16) for x in inverses]
            moved = [
                dot(jnp.where(below, system, 0.0).astype(BF16), x).astype(BF16)
                for system, x in zip(systems, short_inv)
            ]
            inverses = [
                x - dot(s, m) for x, s, m in zip(inverses, short_inv, moved)
            ]
        else:
            short_inv = [x.astype(BF16) for x in inverses]
            moved = [
                dot(system[size:, :size].astype(BF16), x[:size, :size]).astype(BF16)
                for system, x in zip(systems, short_inv)
            ]
            corner = [dot(x[size:, size:], m) for x, m in zip(short_inv, moved)]
            inverses = [
                jnp.concatenate(
                    [x[:size], jnp.concatenate([-c, x[size:, size:]], axis=1)], axis=0
                )
                for x, c in zip(inverses, corner)
            ]
        size *= 2
    return inverses


def prep_kernel(per_step, blocks_ref, q_ref, k_ref, v_ref, rows_ref, core_ref, final_ref):
    step = pl.program_id(0)
    tokens = TAIL_POSITIONS
    square = (tokens, tokens)
    row, col = iota(square, 0), iota(square, 1)
    upto = jnp.where(row <= col, 1.0, 0.0)
    within = row >= col
    strict = row > col
    scale = WIDTH ** (-0.5)

    masked = []
    for r in range(per_step):
        live = iota((4, tokens), 1) < blocks_ref[step * per_step + r] * BLOCK
        masked.append(jnp.where(live, rows_ref[0, :, r * tokens : (r + 1) * tokens], 0.0))
    masked = jnp.concatenate(masked, axis=0)
    running = lax.dot_general(
        masked, upto, (((1,), (0,)), ((), ())), precision=HIGHEST, preferred_element_type=F32
    )
    tall = jnp.transpose(jnp.concatenate([masked, running], axis=0))

    keys, queries, systems, fades, scores = [], [], [], [], []
    for r in range(per_step):
        span = pl.ds(r * tokens, tokens)
        k = unit_rows(k_ref[span, :]).astype(BF16)
        q = (unit_rows(q_ref[span, :]) * scale).astype(BF16)
        keys.append(k)
        queries.append(q)
        pair = dot(jnp.concatenate([k, q], axis=0), k, ((1,), (1,)))
        for h in range(2):
            at = r * 4 + 2 + h
            run_row = running[at : at + 1]
            run_col = tall[:, per_step * 4 + at : per_step * 4 + at + 1]
            rate_col = tall[:, r * 4 + h : r * 4 + h + 1]
            fade = jnp.exp(jnp.where(within, run_col - run_row, -1e30))
            systems.append(jnp.where(strict, rate_col * pair[:tokens] * fade, 0.0))
            scores.append((pair[tokens:] * fade).astype(BF16))
    inverses = unit_lower_inverse(systems)
    solved = []
    for r in range(per_step):
        key_wide = keys[r].astype(F32)
        for h in range(2):
            i = r * 2 + h
            at = r * 4 + 2 + h
            grow_col = jnp.exp(tall[:, per_step * 4 + at : per_step * 4 + at + 1])
            rate_row = masked[r * 4 + h : r * 4 + h + 1]
            left = (inverses[i] * rate_row).astype(BF16)
            right = jnp.concatenate(
                [
                    v_ref[pl.ds(r * tokens, tokens), h * WIDTH : (h + 1) * WIDTH],
                    (key_wide * grow_col).astype(BF16),
                ],
                axis=1,
            )
            solved.append(dot(left, right).astype(BF16))
    for r in range(per_step):
        key_turned = jnp.transpose(keys[r].astype(F32))
        query_wide = queries[r].astype(F32)
        for h in range(2):
            i = r * 2 + h
            at = r * 4 + 2 + h
            run_row = running[at : at + 1]
            end = run_row[:, tokens - 1 : tokens]
            grow_col = jnp.exp(tall[:, per_step * 4 + at : per_step * 4 + at + 1])
            ending = (key_turned * jnp.exp(end - run_row)).astype(BF16)
            both = dot(jnp.concatenate([scores[i], ending], axis=0), solved[i])
            kept = jnp.where(row == col, jnp.exp(end), 0.0)
            core_ref[r, h, :WIDTH] = (query_wide * grow_col - both[:tokens, WIDTH:]).astype(BF16)
            core_ref[r, h, WIDTH:] = both[:tokens, :WIDTH].astype(BF16)
            final_ref[r, h, :WIDTH] = (kept - both[tokens:, WIDTH:]).astype(BF16)
            final_ref[r, h, WIDTH:] = both[tokens:, :WIDTH].astype(BF16)


def prepare(blocks, queries, keys, values, rows):
    requests = blocks.shape[0]
    chunks = rows.shape[0]
    per_step = 8 if requests % 8 == 0 else 4
    span = per_step * TAIL_POSITIONS
    tall = (requests, 2 * chunks, 2 * WIDTH, WIDTH)
    block = pl.BlockSpec((per_step, 2) + tall[2:], lambda s, c, _: (s, c, 0, 0))
    return pl.pallas_call(
        functools.partial(prep_kernel, per_step),
        out_shape=(jax.ShapeDtypeStruct(tall, BF16), jax.ShapeDtypeStruct(tall, BF16)),
        grid_spec=pltpu.PrefetchScalarGridSpec(
            num_scalar_prefetch=1,
            grid=(requests // per_step, chunks),
            in_specs=[
                pl.BlockSpec((span, WIDTH), lambda s, c, _: (s, c)),
                pl.BlockSpec((span, WIDTH), lambda s, c, _: (s, c)),
                pl.BlockSpec((span, 2 * WIDTH), lambda s, c, _: (s, c)),
                pl.BlockSpec((1, 4, span), lambda s, c, _: (c, 0, s)),
            ],
            out_specs=(block, block),
        ),
        compiler_params=params(),
        cost_estimate=pl.CostEstimate(
            flops=requests * 4 * 24 * 2 * 128**3, bytes_accessed=24 << 20, transcendentals=0
        ),
        name="prepare",
    )(blocks, queries, keys, values, rows)


def finish_kernel(owner_ref, state_ref, maps_ref, out_ref, states, maps, finals, state_sems, map_sems, out_sems):
    requests, heads = maps_ref.shape[:2]
    loads = []
    for r in range(requests):
        pair = (
            pltpu.make_async_copy(state_ref.at[owner_ref[r]], states.at[r], state_sems.at[r]),
            pltpu.make_async_copy(maps_ref.at[r], maps.at[r], map_sems.at[r]),
        )
        for load in pair:
            load.start()
        loads.append(pair)
    stores = []
    for r in range(requests):
        for load in loads[r]:
            load.wait()
        for h in range(heads):
            moved = dot(maps[r, h, :WIDTH], states[r, h])
            finals[r, h] = (moved + maps[r, h, WIDTH:].astype(F32)).astype(BF16)
        store = pltpu.make_async_copy(finals.at[r], out_ref.at[owner_ref[r]], out_sems.at[r])
        store.start()
        stores.append(store)
    for store in stores:
        store.wait()


def finish(owners, states, maps):
    requests = maps.shape[0]
    one = states.shape[1:]
    return pl.pallas_call(
        finish_kernel,
        out_shape=jax.ShapeDtypeStruct(states.shape, BF16),
        grid_spec=pltpu.PrefetchScalarGridSpec(
            num_scalar_prefetch=1,
            grid=(1,),
            in_specs=[pl.BlockSpec(memory_space=pl.ANY)] * 2,
            out_specs=pl.BlockSpec(memory_space=pl.ANY),
            scratch_shapes=[
                pltpu.VMEM((requests,) + one, BF16),
                pltpu.VMEM(maps.shape, BF16),
                pltpu.VMEM((requests,) + one, BF16),
                pltpu.SemaphoreType.DMA((requests,)),
                pltpu.SemaphoreType.DMA((requests,)),
                pltpu.SemaphoreType.DMA((requests,)),
            ],
        ),
        compiler_params=params(),
        cost_estimate=pl.CostEstimate(
            flops=requests * 4 * 2 * 128**3, bytes_accessed=13 << 20, transcendentals=0
        ),
        name="finish",
    )(owners, states, maps)


def block_at(step, group_ref, group_steps, groups, shifts):
    shift = shifts[-1]
    for i in range(len(shifts) - 1):
        shift = jnp.where(step // group_steps == i, shifts[i], shift)
    return ((group_ref[0] + shift) % groups) * group_steps + step % group_steps


def emit_kernel(per_step, group_steps, groups, shifts, owner_ref, blocks_ref, group_ref, *refs):
    state_refs = refs[:per_step]
    maps_ref, gate_ref, gain_ref = refs[per_step : per_step + 3]
    out_refs = refs[per_step + 3 :]
    step = pl.program_id(0)
    first = block_at(step, group_ref, group_steps, groups, shifts) * per_step
    tokens = TAIL_POSITIONS
    heads = maps_ref.shape[1]
    gain = gain_ref[...]
    rows = []
    for r in range(per_step):
        live = iota((tokens, WIDTH), 0) < blocks_ref[first + r] * BLOCK
        parts = []
        for h in range(heads):
            core = dot(maps_ref[r, h, :WIDTH], state_refs[r][0, h]) + maps_ref[r, h, WIDTH:].astype(F32)
            gate = gate_ref[pl.ds(r * tokens, tokens), h * WIDTH : (h + 1) * WIDTH].astype(F32)
            spread = jnp.mean(core * core, axis=-1, keepdims=True)
            normed = core * lax.rsqrt(spread + EPSILON) * gain * (gate / (1.0 + jnp.exp(-gate)))
            parts.append(jnp.where(live, normed, 0.0).astype(BF16))
        rows.append(jnp.concatenate(parts, axis=1))
    for i in range(len(shifts)):

        @pl.when(step // group_steps == i)
        def _(i=i):
            for r in range(per_step):
                out_refs[i][pl.ds(r * tokens, tokens), :] = rows[r]


def emit(owners, blocks, group, groups, shifts, states, maps, gates, gain):
    requests = blocks.shape[0]
    share = requests // groups
    per_step = 6 if share % 6 == 0 else 1
    group_steps = share // per_step
    span = per_step * TAIL_POSITIONS
    heads = maps.shape[1]

    def at(step, group_ref):
        return block_at(step, group_ref, group_steps, groups, shifts)

    def state_spec(r):
        return pl.BlockSpec(
            (1,) + states.shape[1:], lambda s, o, b, g: (o[at(s, g) * per_step + r], 0, 0, 0)
        )

    def out_spec(i):
        return pl.BlockSpec(
            (span, heads * WIDTH),
            lambda s, o, b, g: (jnp.clip(s - i * group_steps, 0, group_steps - 1), 0),
        )

    return pl.pallas_call(
        functools.partial(emit_kernel, per_step, group_steps, groups, shifts),
        out_shape=[
            jax.ShapeDtypeStruct((share * TAIL_POSITIONS, heads * WIDTH), BF16)
            for _ in shifts
        ],
        grid_spec=pltpu.PrefetchScalarGridSpec(
            num_scalar_prefetch=3,
            grid=(len(shifts) * group_steps,),
            in_specs=[state_spec(r) for r in range(per_step)]
            + [
                pl.BlockSpec((per_step,) + maps.shape[1:], lambda s, o, b, g: (at(s, g), 0, 0, 0)),
                pl.BlockSpec((span, heads * WIDTH), lambda s, o, b, g: (at(s, g), 0)),
                pl.BlockSpec((1, WIDTH), lambda s, o, b, g: (0, 0)),
            ],
            out_specs=[out_spec(i) for i in range(len(shifts))],
        ),
        compiler_params=params(),
        cost_estimate=pl.CostEstimate(
            flops=requests * 4 * 2 * 128**3, bytes_accessed=16 << 20, transcendentals=0
        ),
        name="emit",
    )(owners, blocks, group, *([states] * per_step), maps, gates, gain)


def place_kernel(source_ref, arrived_ref, out_ref, short, wide, in_sems, out_sems):
    slots = out_ref.shape[0]
    loads = [
        pltpu.make_async_copy(arrived_ref.at[source_ref[i]], short.at[i], in_sems.at[i])
        for i in range(slots)
    ]
    for load in loads:
        load.start()
    stores = []
    for i in range(slots):
        loads[i].wait()
        wide[i] = short[i].astype(F32)
        store = pltpu.make_async_copy(wide.at[i], out_ref.at[i], out_sems.at[i])
        store.start()
        stores.append(store)
    for store in stores:
        store.wait()


def place(source, arrived):
    slots = source.shape[0]
    shape = (slots,) + arrived.shape[1:]
    return pl.pallas_call(
        place_kernel,
        out_shape=jax.ShapeDtypeStruct(shape, F32),
        grid_spec=pltpu.PrefetchScalarGridSpec(
            num_scalar_prefetch=1,
            grid=(1,),
            in_specs=[pl.BlockSpec(memory_space=pl.ANY)],
            out_specs=pl.BlockSpec(memory_space=pl.ANY),
            scratch_shapes=[
                pltpu.VMEM(shape, BF16),
                pltpu.VMEM(shape, F32),
                pltpu.SemaphoreType.DMA((slots,)),
                pltpu.SemaphoreType.DMA((slots,)),
            ],
        ),
        compiler_params=params(),
        cost_estimate=pl.CostEstimate(flops=0, bytes_accessed=10 << 20, transcendentals=0),
        name="place",
    )(source, arrived)


def project_kernel(count, half, place_ref, *refs):
    shares, nears, fars = (refs[i * count : (i + 1) * count] for i in range(3))
    out_ref = refs[-1]
    total = refs[-2][...].astype(F32) if len(refs) > 1 + 3 * count else None
    near_at = pl.multiple_of(place_ref[0] * half, half)
    far_at = pl.multiple_of((1 - place_ref[0]) * half, half)
    for share, near, far in zip(shares, nears, fars):
        for weight, at in ((near, near_at), (far, far_at)):
            term = dot(share[:, pl.ds(at, half)], weight[...])
            total = term if total is None else total + term
    out_ref[...] = total.astype(BF16)


def project(core, shares, nears, fars, earlier):
    rows, width = shares[0].shape
    half = width // 2
    model = nears[0].shape[1]
    tile = min(512, model)

    def weight_spec(weight, far):
        if weight.shape[0] == half:
            return pl.BlockSpec((half, tile), lambda n, _: (0, n))
        return pl.BlockSpec((half, tile), lambda n, c: ((1 - c[0]) if far else c[0], n))

    out_spec = pl.BlockSpec((rows, tile), lambda n, _: (0, n))
    more = [] if earlier is None else [earlier]
    return pl.pallas_call(
        functools.partial(project_kernel, len(shares), half),
        out_shape=jax.ShapeDtypeStruct((rows, model), BF16),
        grid_spec=pltpu.PrefetchScalarGridSpec(
            num_scalar_prefetch=1,
            grid=(model // tile,),
            in_specs=[pl.BlockSpec(a.shape, lambda n, _: (0, 0)) for a in shares]
            + [weight_spec(w, False) for w in nears]
            + [weight_spec(w, True) for w in fars]
            + [out_spec] * len(more),
            out_specs=out_spec,
        ),
        compiler_params=params(),
        cost_estimate=pl.CostEstimate(
            flops=4 * rows * len(shares) * half * model, bytes_accessed=12 << 20, transcendentals=0
        ),
        name="project",
    )(core, *shares, *nears, *fars, *more)


def local(
    queries,
    key_rows,
    values,
    gate_input,
    write_rate,
    log_decay,
    norm_gain,
    out_weight,
    cache_states,
    cache_owner,
    cache_slot,
    suffix_blocks,
    new_slot,
):
    owner_count = lax.axis_size("req")
    groups = lax.axis_size("head")
    device = lax.axis_index("req")
    tokens = queries.shape[0]
    requests = tokens // TAIL_POSITIONS
    heads_all = values.shape[1]
    chunks = queries.shape[1]
    heads = heads_all // chunks

    picked = pick_states(device.reshape(1), owner_count, cache_owner, cache_slot, cache_states)
    arrived = lax.all_to_all(picked, "req", split_axis=0, concat_axis=0, tiled=True)

    my_owner = lax.dynamic_slice_in_dim(cache_owner, device * requests, requests)
    my_blocks = lax.dynamic_slice_in_dim(suffix_blocks, device * requests, requests)
    naming = cache_owner.reshape(owner_count, requests) == device
    slot_ids = jnp.arange(requests, dtype=jnp.int32)
    claimed = naming[None] & (
        new_slot.reshape(owner_count, requests)[None] == slot_ids[:, None, None]
    )
    device_ids = jnp.arange(owner_count, dtype=jnp.int32)[None, :, None]
    source = jnp.sum(jnp.where(claimed, device_ids, 0), axis=(1, 2))

    query_flat = queries.reshape(tokens, -1)
    key_flat = key_rows.reshape(tokens, -1)
    value_flat = values.reshape(tokens, -1)
    gate_flat = gate_input.reshape(tokens, -1)
    half = out_weight.shape[0] // 2
    core = device % 2
    out_weight, my_owner = lax.optimization_barrier((out_weight, my_owner))
    own_rows = lax.dynamic_slice_in_dim(out_weight, core * half, half)
    nears = [
        lax.ppermute(own_rows, "head", [(i, (i + d) % groups) for i in range(groups)])
        for d in range(1, groups)
    ]
    rows = jnp.concatenate(
        [
            write_rate.T.reshape(chunks, heads, tokens),
            log_decay.T.reshape(chunks, heads, tokens),
        ],
        axis=1,
    )
    gain = norm_gain.reshape(1, -1)

    core_maps, final_maps = prepare(my_blocks, query_flat, key_flat, value_flat, rows)
    gate_flat, my_owner, nears, arrived, final_maps = lax.optimization_barrier(
        (gate_flat, my_owner, nears, arrived, final_maps)
    )
    swap = [(i, i ^ 1) for i in range(owner_count)]
    fars = [lax.ppermute(w, "req", swap) for w in nears]
    final = finish(my_owner, arrived, final_maps)
    fars, final = lax.optimization_barrier((fars, final))
    returned = lax.all_to_all(final, "req", split_axis=0, concat_axis=0, tiled=True)
    group = lax.axis_index("head")
    shares = [None] * groups
    order = sorted(range(groups), key=lambda d: -min(d, groups - d))
    for shifts in (order[:1], order[1:]):
        made = emit(
            my_owner, my_blocks, group.reshape(1), groups, shifts, arrived, core_maps, gate_flat, gain
        )
        for d, share in zip(shifts, made):
            pairs = [(i, (i + d) % groups) for i in range(groups)]
            shares[d] = lax.ppermute(share, "head", pairs) if d else share
    early, late = order[:1] + order[-1:], order[1:-1]
    layer_out = None
    for shifts in (early, late):
        if shifts:
            weights = [[[out_weight, *part][d] for d in shifts] for part in (nears, fars)]
            taken = [[shares[d] for d in shifts], *weights]
            layer_out = project(core.reshape(1), *taken, layer_out)
    returned, layer_out = lax.optimization_barrier((returned, layer_out))
    new_cache = place(source, returned)
    return (layer_out, new_cache)


def solution(mesh):
    return jax.shard_map(
        local,
        mesh=mesh,
        in_specs=(
            P("req", "head", None),
            P("req", "head", None),
            P("req", "head", None),
            P("req", "head", None),
            P("req", "head"),
            P("req", "head"),
            P(),
            P("head", None),
            P("req", "head", None, None),
            P(),
            P(),
            P(),
            P(),
        ),
        out_specs=(P(("req", "head"), None), P("req", "head", None, None)),
        check_vma=False,
    )
```
